32 devices in a mesh: grp: 4 (over y, x), dom: 8 (over z, core).
Axes of the slice: x: 2, y: 2, z: 4, core: 2. Of those that a mesh axis runs over, the one named last changes fastest.
Arguments:
- fine_matrix_blocks: bfloat16 [2048, 64, 768], P(('grp', 'dom')), may hold values from -0.21875 to 0.21875
- prolongator: bfloat16 [2048, 64, 64], P(('grp', 'dom')), may hold values from -1.5 to 1.5
- block_columns: int32 [2048, 12], P(('grp', 'dom')), may hold values from 0 to 2047, as said below
- block_aggregates: int32 [2048, 12], P(('grp', 'dom')), may hold values from 0 to 127, as said below
- live_counts: int32 [32], P(('grp', 'dom')), may hold values from 16 to 64, as said below
Outputs:
- coarse_operator: float32 [128, 64, 768], P('dom')
The draws below stay inside these ranges and needn't reach their ends.
Inputs may be any that keep to these rules, and one draw needn't show every extreme that they name: live_counts[p] counts the first slots of partition p that hold block rows; some partition has 64 and some has 16. `block_columns`: entry 0 of row i is i itself. For a live row of partition p, every entry is a live row of partition p - 1, p or p + 1 (only partitions that exist); entries may repeat, and repeated blocks add. block_aggregates[i, k] is the aggregate of row block_columns[i, k]. Every row of partition p, with g = p // 8 and q = p % 8, has an aggregate from (((q + 2 * g) % 8) * 4 + g) * 4 to that number plus 4 - 1.
All inputs are finite; a program needn't handle non-finite values.
Results may differ from the reference program's by a relative error of at most 0.0029.
Values may be sent and summed in bfloat16 or wider, within the bound.
A program may use at most 192 MiB of HBM per device.

```python
import jax
import jax.numpy as jnp
from jax import lax

BLOCK_ORDER = 64
ROW_BLOCK_COUNT = 12
CAP = 64
AGG_DEV = 4
GROUP_COUNT = 4
GROUP_PARTS = 8
GROUP_STRIDE = 2
SLOT_COUNT = 2048
COARSE = 128


def layout(key):
    partitions = GROUP_COUNT * GROUP_PARTS
    slot_total = CAP * partitions
    subkeys = jax.random.split(jax.random.fold_in(key, 7), 5)
    counts = jax.random.randint(subkeys[0], (partitions,), CAP // 4, CAP + 1)
    busiest = jax.random.randint(subkeys[1], (), 0, partitions)
    positions = jnp.arange(partitions)
    counts = jnp.where(positions == busiest, CAP, counts)
    counts = jnp.where(positions == (busiest + 1) % partitions, CAP // 4, counts)
    own_part = jnp.arange(slot_total) // CAP
    rolled = jax.random.randint(subkeys[2], (slot_total, ROW_BLOCK_COUNT), 0, 10)
    offsets = jnp.where(rolled < 2, -1, jnp.where(rolled >= 8, 1, 0))
    target = own_part[:, None] + offsets
    target = jnp.where((target < 0) | (target >= partitions), own_part[:, None], target)
    drawn_slots = jax.random.randint(subkeys[3], (slot_total, ROW_BLOCK_COUNT), 0, 1048576)
    columns_drawn = target * CAP + drawn_slots % counts[target]
    columns_drawn = columns_drawn.at[:, 0].set(jnp.arange(slot_total))
    local_agg = jax.random.randint(subkeys[4], (slot_total,), 0, AGG_DEV)
    group_index = own_part // GROUP_PARTS
    place_index = own_part % GROUP_PARTS
    first_id = ((place_index + GROUP_STRIDE * group_index) % GROUP_PARTS * GROUP_COUNT + group_index) * AGG_DEV
    row_agg = first_id + local_agg
    return (counts.astype(jnp.int32), columns_drawn.astype(jnp.int32), row_agg[columns_drawn].astype(jnp.int32))


def draw_live_counts(key, part):
    return layout(key)[0]


def draw_block_columns(key, part):
    return layout(key)[1]


def draw_block_aggregates(key, part):
    return layout(key)[2]


def block_levels(own_key, extent, cuts, low, high):
    gain, own = 1.0, jax.random.fold_in(own_key, 6)
    for dim, shards_of in cuts:
        heights = jnp.exp(jax.random.uniform(jax.random.fold_in(own, dim), (shards_of,), jnp.float32, low / len(cuts), high / len(cuts)))
        gain = gain * jnp.repeat(heights, extent[dim] // shards_of).reshape([-1 if axis == dim else 1 for axis in range(len(extent))])
    return gain


def centred(key, shape, width, limit, shards=(), kind=jnp.bfloat16):
    array = jax.random.normal(key, shape, jnp.float32) * width
    if len(shards) > 0:
        array = block_levels(key, shape, shards, -0.22, 0.18) * array
    return jnp.clip(array, min=-limit, max=limit).astype(kind)


def setup_inputs(seed: int = 0) -> dict:
    keys = jax.random.split(jax.random.key(seed), 6)
    return {
        "fine_matrix_blocks": centred(keys[0], (SLOT_COUNT, BLOCK_ORDER, ROW_BLOCK_COUNT * BLOCK_ORDER), (ROW_BLOCK_COUNT * BLOCK_ORDER) ** -0.5, 0.21875, ((0, 32),)),
        "prolongator": centred(keys[1], (SLOT_COUNT, BLOCK_ORDER, BLOCK_ORDER), 16 ** -0.5, 1.5, ((0, 32),)),
        "block_columns": draw_block_columns(jax.random.fold_in(keys[5], 71), 0),
        "block_aggregates": draw_block_aggregates(jax.random.fold_in(keys[5], 71), 0),
        "live_counts": draw_live_counts(jax.random.fold_in(keys[5], 71), 0),
    }


def reference(fine_matrix_blocks, prolongator, block_columns, block_aggregates, live_counts):
    partitions = GROUP_COUNT * GROUP_PARTS
    slot_width = 3 * AGG_DEV
    matrix_view = fine_matrix_blocks.reshape(SLOT_COUNT, BLOCK_ORDER, ROW_BLOCK_COUNT, BLOCK_ORDER)

    def one_partition(partition):
        start = (partition * CAP).astype(jnp.int32)
        block_rows = lax.dynamic_slice_in_dim(matrix_view, start, CAP, 0).astype(jnp.float32)
        columns = lax.dynamic_slice_in_dim(block_columns, start, CAP, 0)
        aggregates = lax.dynamic_slice_in_dim(block_aggregates, start, CAP, 0)
        own_blocks = lax.dynamic_slice_in_dim(prolongator, start, CAP, 0).astype(jnp.float32)
        gathered = prolongator[columns].astype(jnp.float32)
        products = jnp.einsum("ixky,ikyz->ixkz", block_rows, gathered, precision=lax.Precision.HIGHEST)
        coarse_slot = AGG_DEV * (columns // CAP - partition + 1) + aggregates % AGG_DEV
        live_rows = (jnp.arange(CAP) < live_counts[partition]).astype(jnp.float32)
        slot_select = (coarse_slot[:, :, None] == jnp.arange(slot_width)[None, None, :]).astype(jnp.float32)
        slot_select = slot_select * live_rows[:, None, None]
        row_sums = jnp.einsum("ikt,ixkz->ixtz", slot_select, products, precision=lax.Precision.HIGHEST)
        row_sums = row_sums.astype(jnp.bfloat16).astype(jnp.float32).reshape(CAP * BLOCK_ORDER, slot_width * BLOCK_ORDER)
        row_select = (aggregates[:, 0:1] % AGG_DEV == jnp.arange(AGG_DEV)[None, :]).astype(jnp.float32)
        row_select = row_select * live_rows[:, None]
        spread = (row_select[:, None, :, None] * own_blocks[:, :, None, :]).reshape(CAP * BLOCK_ORDER, AGG_DEV * BLOCK_ORDER)
        coarse = jnp.dot(spread.T, row_sums, precision=lax.Precision.HIGHEST, preferred_element_type=jnp.float32)
        first_block = aggregates[0, 0] // AGG_DEV
        return coarse.reshape(AGG_DEV, BLOCK_ORDER, slot_width * BLOCK_ORDER), first_block

    coarse_all, first_blocks = lax.map(one_partition, jnp.arange(partitions, dtype=jnp.int32))
    positions = (first_blocks[:, None] * AGG_DEV + jnp.arange(AGG_DEV, dtype=jnp.int32)[None, :]).reshape(-1)
    assembled = jnp.zeros((COARSE, BLOCK_ORDER, slot_width * BLOCK_ORDER), jnp.float32)
    assembled = assembled.at[positions].set(coarse_all.reshape(partitions * AGG_DEV, BLOCK_ORDER, slot_width * BLOCK_ORDER))
    return assembled
```

```python
import functools

import jax
import jax.numpy as jnp
from jax import lax
from jax.experimental import pallas as pl
from jax.experimental.pallas import tpu as pltpu
from jax.sharding import PartitionSpec as P

AGG_DEV = 4
BF = jnp.bfloat16
F32 = jnp.float32


def fill_masks(mask):
    sides, codes, tiles, rows, lanes = mask.shape
    lane = lax.broadcasted_iota(jnp.int32, (rows, lanes), 1)
    high = (lane >= lanes // 2).astype(jnp.int32)
    for s in range(sides):
        for m in range(tiles):
            slot = AGG_DEV * s + 2 * m + high

            def fill(c, _):
                mask[s, c, m] = (slot == c).astype(F32).astype(BF)
                return 0

            lax.fori_loop(0, codes, fill, 0)


def masked(block, mask):
    repeat = block.shape[0] // mask.shape[0]
    return block * jnp.concatenate([mask] * repeat, axis=0)


def both(x):
    return jnp.concatenate([x, x], axis=-1)


def dup_packed(packed, table):
    half = packed.shape[0]
    width = packed.shape[2] // 2

    def step(j, _):
        x = packed[j]
        table[j] = both(x[:, :width])
        table[j + half] = both(x[:, width:])
        return 0

    lax.fori_loop(0, half, step, 0)


def row_pass(side, code, fine, table, mask, rows_out):
    capacity, width, _ = fine.shape
    ks = fine.shape[2] // width

    def step(i, _):
        left, right = [], []
        for k in range(ks):
            c = code[i, k]
            row = lax.rem(c, capacity)
            slot = lax.div(c, capacity)
            block = table[row]
            left.append(masked(block, mask[side, slot, 0]))
            right.append(masked(block, mask[side, slot, 1]))
        weights = jnp.concatenate(
            [jnp.concatenate(left, axis=0), jnp.concatenate(right, axis=0)], axis=1
        )
        sums = jnp.dot(fine[i], weights, preferred_element_type=F32)
        rows_out[pl.ds(pl.multiple_of(i * width, width), width), :] = sums.astype(BF)
        return 0

    lax.fori_loop(0, capacity, step, 0, unroll=2)


def spread_pass(code, table, mask, spread):
    capacity, width, _ = table.shape

    def step(i, _):
        slot = lax.div(code[i, 0], capacity)
        block = table[i]
        value = jnp.concatenate(
            [masked(block, mask[1, slot, 0]), masked(block, mask[1, slot, 1])], axis=1
        )
        spread[pl.ds(pl.multiple_of(i * width, width), width), :] = value
        return 0

    lax.fori_loop(0, capacity, step, 0, unroll=2)


def coarse_pass(spread, rows, total):
    depth = 1024
    for step in range(spread.shape[0] // depth):
        part = lax.dot_general(
            spread[pl.ds(step * depth, depth), :],
            rows[pl.ds(step * depth, depth), :],
            (((0,), (0,)), ((), ())),
            preferred_element_type=F32,
        )
        if step == 0:
            total[...] = part
        else:
            total[...] += part


def kernel(code, fine, own, low, high, out, t_low, t_own, t_high, mask, rows, spread, total):
    fill_masks(mask)

    def step(j, _):
        t_own[j] = both(own[j])
        return 0

    lax.fori_loop(0, own.shape[0], step, 0)
    dup_packed(low, t_low)
    dup_packed(high, t_high)
    spread_pass(code, t_own, mask, spread)
    for side, table in ((1, t_own), (0, t_low), (2, t_high)):
        row_pass(side, code, fine, table, mask, rows)
        coarse_pass(spread, rows, total)
        width = total.shape[1]
        out[:, side * width : (side + 1) * width] = total[...].astype(BF)


def local(fine_matrix_blocks, prolongator, block_columns, block_aggregates, live_counts):
    capacity, width, wide = fine_matrix_blocks.shape
    groups = lax.axis_size("grp")
    doms = lax.axis_size("dom")
    stride = doms // groups
    position = lax.axis_index(("grp", "dom"))
    slots = 3 * AGG_DEV
    half = capacity // 2
    packed = jnp.concatenate([prolongator[:half], prolongator[half:]], axis=-1)
    count = groups * doms
    low = lax.ppermute(packed, ("grp", "dom"), [(i, (i + 1) % count) for i in range(count)])
    high = lax.ppermute(packed, ("grp", "dom"), [((i + 1) % count, i) for i in range(count)])
    slot = AGG_DEV * (block_columns // capacity - position + 1) + block_aggregates % AGG_DEV
    live = (jnp.arange(capacity) < live_counts[0])[:, None]
    code = jnp.where(live, slot, slots) * capacity + block_columns % capacity
    lanes = 2 * width
    both_w = AGG_DEV * width
    coarse = pl.pallas_call(
        kernel,
        out_shape=jax.ShapeDtypeStruct((both_w, 3 * both_w), BF),
        in_specs=[pl.BlockSpec(memory_space=pltpu.SMEM)]
        + [pl.BlockSpec(memory_space=pltpu.VMEM)] * 4,
        out_specs=pl.BlockSpec(memory_space=pltpu.VMEM),
        scratch_shapes=[
            pltpu.VMEM((capacity, width, lanes), BF),
            pltpu.VMEM((capacity, width, lanes), BF),
            pltpu.VMEM((capacity, width, lanes), BF),
            pltpu.VMEM((3, slots + 1, 2, 16, lanes), BF),
            pltpu.VMEM((capacity * width, both_w), BF),
            pltpu.VMEM((capacity * width, both_w), BF),
            pltpu.VMEM((both_w, both_w), F32),
        ],
        compiler_params=pltpu.CompilerParams(vmem_limit_bytes=48 * 2**20),
    )(code, fine_matrix_blocks, prolongator, low, high)
    moves = [
        (g * doms + q, g * doms + (q + stride * g) % doms)
        for g in range(groups)
        for q in range(doms)
    ]
    moved = lax.ppermute(coarse, ("grp", "dom"), moves)
    result = lax.all_gather(moved, "grp", axis=0, tiled=True)
    return result.astype(F32).reshape(groups * AGG_DEV, width, 3 * both_w)


def solution(mesh):
    return jax.shard_map(
        local,
        mesh=mesh,
        in_specs=(
            P(("grp", "dom"), None, None),
            P(("grp", "dom"), None, None),
            P(("grp", "dom"), None),
            P(("grp", "dom"), None),
            P(("grp", "dom")),
        ),
        out_specs=P("dom", None, None),
        check_vma=False,
    )
```

```python
import functools

import jax
import jax.numpy as jnp
from jax import lax
from jax.experimental import pallas as pl
from jax.experimental.pallas import tpu as pltpu
from jax.sharding import PartitionSpec as P

AGG_DEV = 4
BF = jnp.bfloat16
F32 = jnp.float32


def fill_masks(mask):
    sides, codes, tiles, rows, lanes = mask.shape
    lane = lax.broadcasted_iota(jnp.int32, (rows, lanes), 1)
    high = (lane >= lanes // 2).astype(jnp.int32)
    for s in range(sides):
        for m in range(tiles):
            slot = AGG_DEV * s + 2 * m + high

            def fill(c, _):
                mask[s, c, m] = (slot == c).astype(F32).astype(BF)
                return 0

            lax.fori_loop(0, codes, fill, 0)


def masked(block, mask):
    repeat = block.shape[0] // mask.shape[0]
    return block * jnp.concatenate([mask] * repeat, axis=0)


def both(x):
    return jnp.concatenate([x, x], axis=-1)


def dup_packed(packed, table):
    half = packed.shape[0]
    width = packed.shape[2] // 2

    def step(j, _):
        x = packed[j]
        table[j] = both(x[:, :width])
        table[j + half] = both(x[:, width:])
        return 0

    lax.fori_loop(0, half, step, 0)


def row_pass(side, code, fine, table, mask, rows_out, first, count):
    capacity, width, _ = fine.shape
    ks = fine.shape[2] // width

    def step(i, _):
        left, right = [], []
        for k in range(ks):
            c = code[i, k]
            row = lax.rem(c, capacity)
            slot = lax.div(c, capacity)
            block = table[row]
            left.append(masked(block, mask[side, slot, 0]))
            right.append(masked(block, mask[side, slot, 1]))
        weights = jnp.concatenate(
            [jnp.concatenate(left, axis=0), jnp.concatenate(right, axis=0)], axis=1
        )
        sums = jnp.dot(fine[i], weights, preferred_element_type=F32)
        rows_out[pl.ds(pl.multiple_of(i * width, width), width), :] = sums.astype(BF)
        return 0

    lax.fori_loop(first, first + count, step, 0)


def spread_pass(code, table, mask, spread):
    capacity, width, _ = table.shape

    def step(i, _):
        slot = lax.div(code[i, 0], capacity)
        block = table[i]
        value = jnp.concatenate(
            [masked(block, mask[1, slot, 0]), masked(block, mask[1, slot, 1])], axis=1
        )
        spread[pl.ds(pl.multiple_of(i * width, width), width), :] = value
        return 0

    lax.fori_loop(0, capacity, step, 0)


def coarse_pass(spread, rows, total):
    depth = 1024
    for step in range(spread.shape[0] // depth):
        part = lax.dot_general(
            spread[pl.ds(step * depth, depth), :],
            rows[pl.ds(step * depth, depth), :],
            (((0,), (0,)), ((), ())),
            preferred_element_type=F32,
        )
        if step == 0:
            total[...] = part
        else:
            total[...] += part


def place(index, groups, doms):
    index = lax.rem(index + groups * doms, groups * doms)
    return {"grp": lax.div(index, doms), "dom": lax.rem(index, doms)}


def remote(src, dst, send, recv, device):
    return pltpu.make_async_remote_copy(
        src_ref=src,
        dst_ref=dst,
        send_sem=send,
        recv_sem=recv,
        device_id=device,
        device_id_type=pl.DeviceIdType.MESH,
    )


def kernel(
    groups, doms, code, fine_hbm, own, out,
    fine, packed, low, high, t_low, t_own, t_high, mask, rows, spread, total, mine, landed,
    load_sem, halo_send, halo_recv, shift_send, shift_recv, share_send, share_recv, keep_sem,
):
    capacity, width, _ = own.shape
    half = capacity // 2
    group = lax.axis_index("grp")
    dom = lax.axis_index("dom")
    position = group * doms + dom
    stride = doms // groups
    nearby = [place(position + 1, groups, doms), place(position - 1, groups, doms)]
    target = {"grp": group, "dom": lax.rem(dom + stride * group, doms)}
    source = {"grp": group, "dom": lax.rem(dom + doms - stride * group, doms)}
    peers = [{"grp": lax.rem(group + r, groups), "dom": dom} for r in range(1, groups)]
    barrier = pltpu.get_barrier_semaphore()

    def greet(device):
        pl.semaphore_signal(barrier, inc=1, device_id=device, device_id_type=pl.DeviceIdType.MESH)

    for device in nearby + peers:
        greet(device)

    @pl.when(group > 0)
    def _():
        greet(target)
        greet(source)

    pieces = load_sem.shape[0]
    piece = capacity // pieces
    loads = [
        pltpu.make_async_copy(
            fine_hbm.at[pl.ds(n * piece, piece)], fine.at[pl.ds(n * piece, piece)], load_sem.at[n]
        )
        for n in range(pieces)
    ]
    for load in loads:
        load.start()

    def pack(j, _):
        packed[j] = jnp.concatenate([own[j], own[j + half]], axis=-1)
        return 0

    lax.fori_loop(0, half, pack, 0)
    met = len(nearby) + len(peers)
    pl.semaphore_wait(barrier, jnp.where(group > 0, met + 2, met))

    halos = [
        remote(packed, dst, halo_send.at[n], halo_recv.at[n], nearby[n])
        for n, dst in enumerate((low, high))
    ]
    for halo in halos:
        halo.start()

    fill_masks(mask)

    def step(j, _):
        t_own[j] = both(own[j])
        return 0

    lax.fori_loop(0, capacity, step, 0)
    spread_pass(code, t_own, mask, spread)
    tile = total.shape[1]
    mine_rows = pl.ds(group * AGG_DEV, AGG_DEV)

    def shift(n):
        return remote(mine.at[n], landed.at[n], shift_send.at[n], shift_recv.at[n], target)

    def keep(n, buffer):
        return pltpu.make_async_copy(
            buffer.at[n], out.at[mine_rows, :, pl.ds(n * tile, tile)], keep_sem.at[n]
        )

    def shares(n, buffer):
        return [
            remote(
                buffer.at[n],
                out.at[mine_rows, :, pl.ds(n * tile, tile)],
                share_send.at[n, r],
                share_recv.at[n, r],
                device,
            )
            for r, device in enumerate(peers)
        ]

    def hand_out(n):
        @pl.when(group > 0)
        def _():
            shift(n).wait_recv()
            for copy in [keep(n, landed)] + shares(n, landed):
                copy.start()

        @pl.when(group == 0)
        def _():
            for copy in [keep(n, mine)] + shares(n, mine):
                copy.start()

    order = ((1, t_own), (0, t_low), (2, t_high))
    for place_in_order, (side, table) in enumerate(order):
        if side == 0:
            halos[0].wait_recv()
            dup_packed(low, t_low)
        if side == 2:
            halos[1].wait_recv()
            dup_packed(high, t_high)
        if place_in_order == 0:
            for n in range(pieces):
                loads[n].wait()
                row_pass(side, code, fine, table, mask, rows, n * piece, piece)
        else:
            row_pass(side, code, fine, table, mask, rows, 0, capacity)
        coarse_pass(spread, rows, total)
        mine[side] = total[...].astype(BF).reshape(AGG_DEV, width, tile)

        @pl.when(group > 0)
        def _():
            shift(side).start()

        if place_in_order > 0:
            hand_out(order[place_in_order - 1][0])
    hand_out(order[-1][0])
    for halo in halos:
        halo.wait_send()
    for side, _ in order:
        @pl.when(group > 0)
        def _():
            shift(side).wait_send()

        keep(side, mine).wait()
        for copy in shares(side, mine):
            copy.wait()


def local(fine_matrix_blocks, prolongator, block_columns, block_aggregates, live_counts):
    capacity, width, wide = fine_matrix_blocks.shape
    groups = lax.axis_size("grp")
    doms = lax.axis_size("dom")
    position = lax.axis_index(("grp", "dom"))
    slots = 3 * AGG_DEV
    half = capacity // 2
    slot = AGG_DEV * (block_columns // capacity - position + 1) + block_aggregates % AGG_DEV
    live = (jnp.arange(capacity) < live_counts[0])[:, None]
    code = jnp.where(live, slot, slots) * capacity + block_columns % capacity
    lanes = 2 * width
    tile = AGG_DEV * width
    pieces = 4
    result = pl.pallas_call(
        functools.partial(kernel, groups, doms),
        out_shape=jax.ShapeDtypeStruct((groups * AGG_DEV, width, 3 * tile), BF),
        in_specs=[
            pl.BlockSpec(memory_space=pltpu.SMEM),
            pl.BlockSpec(memory_space=pl.ANY),
            pl.BlockSpec(memory_space=pltpu.VMEM),
        ],
        out_specs=pl.BlockSpec(memory_space=pltpu.VMEM),
        scratch_shapes=[
            pltpu.VMEM((capacity, width, wide), BF),
            pltpu.VMEM((half, width, lanes), BF),
            pltpu.VMEM((half, width, lanes), BF),
            pltpu.VMEM((half, width, lanes), BF),
            pltpu.VMEM((capacity, width, lanes), BF),
            pltpu.VMEM((capacity, width, lanes), BF),
            pltpu.VMEM((capacity, width, lanes), BF),
            pltpu.VMEM((3, slots + 1, 2, 16, lanes), BF),
            pltpu.VMEM((capacity * width, tile), BF),
            pltpu.VMEM((capacity * width, tile), BF),
            pltpu.VMEM((tile, tile), F32),
            pltpu.VMEM((3, AGG_DEV, width, tile), BF),
            pltpu.VMEM((3, AGG_DEV, width, tile), BF),
            pltpu.SemaphoreType.DMA((pieces,)),
            pltpu.SemaphoreType.DMA((2,)),
            pltpu.SemaphoreType.DMA((2,)),
            pltpu.SemaphoreType.DMA((3,)),
            pltpu.SemaphoreType.DMA((3,)),
            pltpu.SemaphoreType.DMA((3, groups - 1)),
            pltpu.SemaphoreType.DMA((3, groups - 1)),
            pltpu.SemaphoreType.DMA((3,)),
        ],
        compiler_params=pltpu.CompilerParams(
            vmem_limit_bytes=48 * 2**20, collective_id=0, has_side_effects=True
        ),
    )(code, fine_matrix_blocks, prolongator)
    return result.astype(F32)


def solution(mesh):
    return jax.shard_map(
        local,
        mesh=mesh,
        in_specs=(
            P(("grp", "dom"), None, None),
            P(("grp", "dom"), None, None),
            P(("grp", "dom"), None),
            P(("grp", "dom"), None),
            P(("grp", "dom")),
        ),
        out_specs=P("dom", None, None),
        check_vma=False,
    )
```

```python
import functools

import jax
import jax.numpy as jnp
from jax import lax
from jax.experimental import pallas as pl
from jax.experimental.pallas import tpu as pltpu
from jax.sharding import PartitionSpec as P

AGG_DEV = 4
BF = jnp.bfloat16
F32 = jnp.float32


def fill_masks(mask):
    sides, codes, tiles, rows, lanes = mask.shape
    lane = lax.broadcasted_iota(jnp.int32, (rows, lanes), 1)
    high = (lane >= lanes // 2).astype(jnp.int32)
    for s in range(sides):
        for m in range(tiles):
            slot = AGG_DEV * s + 2 * m + high

            def fill(c, _):
                mask[s, c, m] = (slot == c).astype(F32).astype(BF)
                return 0

            lax.fori_loop(0, codes, fill, 0)


def masked(block, mask):
    repeat = block.shape[0] // mask.shape[0]
    return block * jnp.concatenate([mask] * repeat, axis=0)


def both(x):
    return jnp.concatenate([x, x], axis=-1)


def dup_packed(packed, table):
    half = packed.shape[0]
    width = packed.shape[2] // 2

    def step(j, _):
        x = packed[j]
        table[j] = both(x[:, :width])
        table[j + half] = both(x[:, width:])
        return 0

    lax.fori_loop(0, half, step, 0)


def row_pass(side, code, fine, table, mask, rows_out, first, count):
    capacity, width, _ = fine.shape
    ks = fine.shape[2] // width

    def step(i, _):
        left, right = [], []
        for k in range(ks):
            c = code[k, i]
            row = lax.rem(c, capacity)
            slot = lax.div(c, capacity)
            block = table[row]
            left.append(masked(block, mask[side, slot, 0]))
            right.append(masked(block, mask[side, slot, 1]))
        weights = jnp.concatenate(
            [jnp.concatenate(left, axis=0), jnp.concatenate(right, axis=0)], axis=1
        )
        sums = jnp.dot(fine[i], weights, preferred_element_type=F32)
        rows_out[pl.ds(pl.multiple_of(i * width, width), width), :] = sums.astype(BF)
        return 0

    lax.fori_loop(first, first + count, step, 0, unroll=4)


def spread_pass(code, table, mask, spread):
    capacity, width, _ = table.shape

    def step(i, _):
        slot = lax.div(code[0, i], capacity)
        block = table[i]
        value = jnp.concatenate(
            [masked(block, mask[1, slot, 0]), masked(block, mask[1, slot, 1])], axis=1
        )
        spread[pl.ds(pl.multiple_of(i * width, width), width), :] = value
        return 0

    lax.fori_loop(0, capacity, step, 0)


def coarse_pass(spread, rows, total):
    depth = 1024
    for step in range(spread.shape[0] // depth):
        part = lax.dot_general(
            spread[pl.ds(step * depth, depth), :],
            rows[pl.ds(step * depth, depth), :],
            (((0,), (0,)), ((), ())),
            preferred_element_type=F32,
        )
        if step == 0:
            total[...] = part
        else:
            total[...] += part


def place(index, groups, doms):
    index = lax.rem(index + groups * doms, groups * doms)
    return {"grp": lax.div(index, doms), "dom": lax.rem(index, doms)}


def remote(src, dst, send, recv, device):
    return pltpu.make_async_remote_copy(
        src_ref=src,
        dst_ref=dst,
        send_sem=send,
        recv_sem=recv,
        device_id=device,
        device_id_type=pl.DeviceIdType.MESH,
    )


def kernel(
    groups, doms, code, fine_hbm, own, out_0, out_1, out_2,
    fine, packed, low, high, t_low, t_own, t_high, mask, rows, spread, total, mine, landed,
    load_sem, halo_send, halo_recv, shift_send, shift_recv, share_send, share_recv, keep_sem,
):
    capacity, width, _ = own.shape
    half = capacity // 2
    group = lax.axis_index("grp")
    dom = lax.axis_index("dom")
    position = group * doms + dom
    stride = doms // groups
    nearby = [place(position + 1, groups, doms), place(position - 1, groups, doms)]
    target = {"grp": group, "dom": lax.rem(dom + stride * group, doms)}
    source = {"grp": group, "dom": lax.rem(dom + doms - stride * group, doms)}
    peers = [{"grp": lax.rem(group + r, groups), "dom": dom} for r in range(1, groups)]
    barrier = pltpu.get_barrier_semaphore()

    def greet(device):
        pl.semaphore_signal(barrier, inc=1, device_id=device, device_id_type=pl.DeviceIdType.MESH)

    for device in nearby + peers:
        greet(device)

    @pl.when(group > 0)
    def _():
        greet(target)
        greet(source)

    pieces = load_sem.shape[0]
    piece = capacity // pieces
    loads = [
        pltpu.make_async_copy(
            fine_hbm.at[pl.ds(n * piece, piece)], fine.at[pl.ds(n * piece, piece)], load_sem.at[n]
        )
        for n in range(pieces)
    ]
    for load in loads:
        load.start()

    def pack(j, _):
        packed[j] = jnp.concatenate([own[j], own[j + half]], axis=-1)
        return 0

    lax.fori_loop(0, half, pack, 0)
    met = len(nearby) + len(peers)
    pl.semaphore_wait(barrier, jnp.where(group > 0, met + 2, met))

    halos = [
        remote(packed, dst, halo_send.at[n], halo_recv.at[n], nearby[n])
        for n, dst in enumerate((low, high))
    ]
    for halo in halos:
        halo.start()

    fill_masks(mask)

    def step(j, _):
        t_own[j] = both(own[j])
        return 0

    lax.fori_loop(0, capacity, step, 0)
    spread_pass(code, t_own, mask, spread)
    tile = total.shape[1]
    outs = (out_0, out_1, out_2)
    mine_rows = pl.ds(group * AGG_DEV, AGG_DEV)

    def shift(n):
        return remote(mine.at[n], landed.at[n], shift_send.at[n], shift_recv.at[n], target)

    def keep(n, buffer):
        return pltpu.make_async_copy(
            buffer.at[n], outs[n].at[mine_rows], keep_sem.at[n]
        )

    def shares(n, buffer):
        return [
            remote(
                buffer.at[n],
                outs[n].at[mine_rows],
                share_send.at[n, r],
                share_recv.at[n, r],
                device,
            )
            for r, device in enumerate(peers)
        ]

    def hand_out(n):
        @pl.when(group > 0)
        def _():
            shift(n).wait_recv()
            for copy in [keep(n, landed)] + shares(n, landed):
                copy.start()

        @pl.when(group == 0)
        def _():
            for copy in [keep(n, mine)] + shares(n, mine):
                copy.start()

    order = ((1, t_own), (0, t_low), (2, t_high))
    for place_in_order, (side, table) in enumerate(order):
        if side == 0:
            halos[0].wait_recv()
            dup_packed(low, t_low)
        if side == 2:
            halos[1].wait_recv()
            dup_packed(high, t_high)
        if place_in_order == 0:
            for n in range(pieces):
                loads[n].wait()
                row_pass(side, code, fine, table, mask, rows, n * piece, piece)
        else:
            cut = 3 * capacity // 4
            row_pass(side, code, fine, table, mask, rows, 0, cut)
            hand_out(order[place_in_order - 1][0])
            row_pass(side, code, fine, table, mask, rows, cut, capacity - cut)
        coarse_pass(spread, rows, total)
        mine[side] = total[...].astype(BF).reshape(AGG_DEV, width, tile)

        @pl.when(group > 0)
        def _():
            shift(side).start()

    hand_out(order[-1][0])
    for halo in halos:
        halo.wait_send()
    for side, _ in order:
        @pl.when(group > 0)
        def _():
            shift(side).wait_send()

        keep(side, mine).wait()
        for copy in shares(side, mine):
            copy.wait()


def local(fine_matrix_blocks, prolongator, block_columns, block_aggregates, live_counts):
    capacity, width, wide = fine_matrix_blocks.shape
    groups = lax.axis_size("grp")
    doms = lax.axis_size("dom")
    position = lax.axis_index(("grp", "dom"))
    slots = 3 * AGG_DEV
    half = capacity // 2
    block_columns, block_aggregates = block_columns.T, block_aggregates.T
    slot = AGG_DEV * (block_columns // capacity - position + 1) + block_aggregates % AGG_DEV
    live = (jnp.arange(capacity) < live_counts[0])[None, :]
    code = jnp.where(live, slot, slots) * capacity + block_columns % capacity
    lanes = 2 * width
    tile = AGG_DEV * width
    pieces = 4
    result = pl.pallas_call(
        functools.partial(kernel, groups, doms),
        out_shape=[jax.ShapeDtypeStruct((groups * AGG_DEV, width, tile), BF)] * 3,
        in_specs=[
            pl.BlockSpec(memory_space=pltpu.SMEM),
            pl.BlockSpec(memory_space=pl.ANY),
            pl.BlockSpec(memory_space=pltpu.VMEM),
        ],
        out_specs=[pl.BlockSpec(memory_space=pltpu.VMEM)] * 3,
        scratch_shapes=[
            pltpu.VMEM((capacity, width, wide), BF),
            pltpu.VMEM((half, width, lanes), BF),
            pltpu.VMEM((half, width, lanes), BF),
            pltpu.VMEM((half, width, lanes), BF),
            pltpu.VMEM((capacity, width, lanes), BF),
            pltpu.VMEM((capacity, width, lanes), BF),
            pltpu.VMEM((capacity, width, lanes), BF),
            pltpu.VMEM((3, slots + 1, 2, 16, lanes), BF),
            pltpu.VMEM((capacity * width, tile), BF),
            pltpu.VMEM((capacity * width, tile), BF),
            pltpu.VMEM((tile, tile), F32),
            pltpu.VMEM((3, AGG_DEV, width, tile), BF),
            pltpu.VMEM((3, AGG_DEV, width, tile), BF),
            pltpu.SemaphoreType.DMA((pieces,)),
            pltpu.SemaphoreType.DMA((2,)),
            pltpu.SemaphoreType.DMA((2,)),
            pltpu.SemaphoreType.DMA((3,)),
            pltpu.SemaphoreType.DMA((3,)),
            pltpu.SemaphoreType.DMA((3, groups - 1)),
            pltpu.SemaphoreType.DMA((3, groups - 1)),
            pltpu.SemaphoreType.DMA((3,)),
        ],
        compiler_params=pltpu.CompilerParams(
            vmem_limit_bytes=48 * 2**20, collective_id=0, has_side_effects=True
        ),
    )(code, fine_matrix_blocks, prolongator)
    return jnp.concatenate([part.astype(F32) for part in result], axis=-1)


def solution(mesh):
    return jax.shard_map(
        local,
        mesh=mesh,
        in_specs=(
            P(("grp", "dom"), None, None),
            P(("grp", "dom"), None, None),
            P(("grp", "dom"), None),
            P(("grp", "dom"), None),
            P(("grp", "dom")),
        ),
        out_specs=P("dom", None, None),
        check_vma=False,
    )
```

```python
import functools

import jax
import jax.numpy as jnp
from jax import lax
from jax.experimental import pallas as pl
from jax.experimental.pallas import tpu as pltpu
from jax.sharding import PartitionSpec as P

AGG_DEV = 4
BF = jnp.bfloat16
F32 = jnp.float32


def fill_masks(mask):
    sides, codes, tiles, rows, lanes = mask.shape
    lane = lax.broadcasted_iota(jnp.int32, (rows, lanes), 1)
    high = (lane >= lanes // 2).astype(jnp.int32)
    for s in range(sides):
        for m in range(tiles):
            slot = AGG_DEV * s + 2 * m + high

            def fill(c, _):
                mask[s, c, m] = (slot == c).astype(F32).astype(BF)
                return 0

            lax.fori_loop(0, codes, fill, 0)


def masked(block, mask):
    repeat = block.shape[0] // mask.shape[0]
    return block * jnp.concatenate([mask] * repeat, axis=0)


def both(x):
    return jnp.concatenate([x, x], axis=-1)


def dup_packed(packed, table):
    half = packed.shape[0]
    width = packed.shape[2] // 2

    def step(j, _):
        x = packed[j]
        table[j] = both(x[:, :width])
        table[j + half] = both(x[:, width:])
        return 0

    lax.fori_loop(0, half, step, 0)


def row_pass(side, code, fine, table, mask, rows_out, first, count):
    capacity, width, _ = fine.shape
    ks = fine.shape[2] // width

    def step(i, _):
        left, right = [], []
        for k in range(ks):
            c = code[k, i]
            row = lax.rem(c, capacity)
            slot = lax.div(c, capacity)
            block = table[row]
            left.append(masked(block, mask[side, slot, 0]))
            right.append(masked(block, mask[side, slot, 1]))
        weights = jnp.concatenate(
            [jnp.concatenate(left, axis=0), jnp.concatenate(right, axis=0)], axis=1
        )
        sums = jnp.dot(fine[i], weights, preferred_element_type=F32)
        rows_out[pl.ds(pl.multiple_of(i * width, width), width), :] = sums.astype(BF)
        return 0

    lax.fori_loop(first, first + count, step, 0, unroll=4)


def spread_pass(code, table, mask, spread):
    capacity, width, _ = table.shape

    def step(i, _):
        slot = lax.div(code[0, i], capacity)
        block = table[i]
        value = jnp.concatenate(
            [masked(block, mask[1, slot, 0]), masked(block, mask[1, slot, 1])], axis=1
        )
        spread[pl.ds(pl.multiple_of(i * width, width), width), :] = value
        return 0

    lax.fori_loop(0, capacity, step, 0)


def coarse_pass(spread, rows, total):
    depth = 1024
    for step in range(spread.shape[0] // depth):
        part = lax.dot_general(
            spread[pl.ds(step * depth, depth), :],
            rows[pl.ds(step * depth, depth), :],
            (((0,), (0,)), ((), ())),
            preferred_element_type=F32,
        )
        if step == 0:
            total[...] = part
        else:
            total[...] += part


def place(index, groups, doms):
    index = lax.rem(index + groups * doms, groups * doms)
    return {"grp": lax.div(index, doms), "dom": lax.rem(index, doms)}


def remote(src, dst, send, recv, device):
    return pltpu.make_async_remote_copy(
        src_ref=src,
        dst_ref=dst,
        send_sem=send,
        recv_sem=recv,
        device_id=device,
        device_id_type=pl.DeviceIdType.MESH,
    )


def kernel(
    groups, doms, code, fine_hbm, own, out_0, out_1, out_2,
    fine, packed, low, high, t_low, t_own, t_high, mask, rows, spread, total, mine, landed,
    load_sem, halo_send, halo_recv, shift_send, shift_recv, share_send, share_recv, keep_sem,
):
    capacity, width, _ = own.shape
    half = capacity // 2
    group = lax.axis_index("grp")
    dom = lax.axis_index("dom")
    position = group * doms + dom
    stride = doms // groups
    nearby = [place(position + 1, groups, doms), place(position - 1, groups, doms)]
    target = {"grp": group, "dom": lax.rem(dom + stride * group, doms)}
    source = {"grp": group, "dom": lax.rem(dom + doms - stride * group, doms)}
    peers = [{"grp": lax.rem(group + r, groups), "dom": dom} for r in range(1, groups)]
    barrier = pltpu.get_barrier_semaphore()

    def greet(device):
        pl.semaphore_signal(barrier, inc=1, device_id=device, device_id_type=pl.DeviceIdType.MESH)

    for device in nearby + peers:
        greet(device)

    @pl.when(group > 0)
    def _():
        greet(target)
        greet(source)

    pieces = load_sem.shape[0]
    piece = capacity // pieces
    loads = [
        pltpu.make_async_copy(
            fine_hbm.at[pl.ds(n * piece, piece)], fine.at[pl.ds(n * piece, piece)], load_sem.at[n]
        )
        for n in range(pieces)
    ]
    for load in loads:
        load.start()

    def pack(j, _):
        packed[j] = jnp.concatenate([own[j], own[j + half]], axis=-1)
        return 0

    lax.fori_loop(0, half, pack, 0)
    met = len(nearby) + len(peers)
    pl.semaphore_wait(barrier, jnp.where(group > 0, met + 2, met))

    halos = [
        remote(packed, dst, halo_send.at[n], halo_recv.at[n], nearby[n])
        for n, dst in enumerate((low, high))
    ]
    for halo in halos:
        halo.start()

    fill_masks(mask)

    def step(j, _):
        t_own[j] = both(own[j])
        return 0

    lax.fori_loop(0, capacity, step, 0)
    spread_pass(code, t_own, mask, spread)
    tile = total.shape[1]
    outs = (out_0, out_1, out_2)
    mine_rows = pl.ds(group * AGG_DEV, AGG_DEV)

    cuts = 2
    span = AGG_DEV // cuts

    def shift(n, h):
        piece = pl.ds(h * span, span)
        return remote(
            mine.at[n, piece],
            landed.at[n, piece],
            shift_send.at[n * cuts + h],
            shift_recv.at[n * cuts + h],
            target,
        )

    def keep(n, buffer):
        return pltpu.make_async_copy(buffer.at[n], outs[n].at[mine_rows], keep_sem.at[n])

    def shares(n, h, buffer):
        return [
            remote(
                buffer.at[n, pl.ds(h * span, span)],
                outs[n].at[pl.ds(group * AGG_DEV + h * span, span)],
                share_send.at[n * cuts + h, r],
                share_recv.at[n * cuts + h, r],
                device,
            )
            for r, device in enumerate(peers)
        ]

    def hand_out(n):
        @pl.when(group > 0)
        def _():
            for h in range(cuts):
                shift(n, h).wait_recv()
                for copy in shares(n, h, landed):
                    copy.start()
            keep(n, landed).start()

        @pl.when(group == 0)
        def _():
            for h in range(cuts):
                for copy in shares(n, h, mine):
                    copy.start()
            keep(n, mine).start()

    order = ((1, t_own), (0, t_low), (2, t_high))
    for place_in_order, (side, table) in enumerate(order):
        if side == 0:
            halos[0].wait_recv()
            dup_packed(low, t_low)
        if side == 2:
            halos[1].wait_recv()
            dup_packed(high, t_high)
        if place_in_order == 0:
            for n in range(pieces):
                loads[n].wait()
                row_pass(side, code, fine, table, mask, rows, n * piece, piece)
        else:
            cut = 3 * capacity // 4
            row_pass(side, code, fine, table, mask, rows, 0, cut)
            hand_out(order[place_in_order - 1][0])
            row_pass(side, code, fine, table, mask, rows, cut, capacity - cut)
        coarse_pass(spread, rows, total)
        mine[side] = total[...].astype(BF).reshape(AGG_DEV, width, tile)

        @pl.when(group > 0)
        def _():
            for h in range(cuts):
                shift(side, h).start()

    hand_out(order[-1][0])
    for halo in halos:
        halo.wait_send()
    for side, _ in order:
        @pl.when(group > 0)
        def _():
            for h in range(cuts):
                shift(side, h).wait_send()

        keep(side, mine).wait()
        for h in range(cuts):
            for copy in shares(side, h, mine):
                copy.wait()


def local(fine_matrix_blocks, prolongator, block_columns, block_aggregates, live_counts):
    capacity, width, wide = fine_matrix_blocks.shape
    groups = lax.axis_size("grp")
    doms = lax.axis_size("dom")
    position = lax.axis_index(("grp", "dom"))
    slots = 3 * AGG_DEV
    half = capacity // 2
    block_columns, block_aggregates = block_columns.T, block_aggregates.T
    slot = AGG_DEV * (block_columns // capacity - position + 1) + block_aggregates % AGG_DEV
    live = (jnp.arange(capacity) < live_counts[0])[None, :]
    code = jnp.where(live, slot, slots) * capacity + block_columns % capacity
    lanes = 2 * width
    tile = AGG_DEV * width
    pieces = 4
    result = pl.pallas_call(
        functools.partial(kernel, groups, doms),
        out_shape=[jax.ShapeDtypeStruct((groups * AGG_DEV, width, tile), BF)] * 3,
        in_specs=[
            pl.BlockSpec(memory_space=pltpu.SMEM),
            pl.BlockSpec(memory_space=pl.ANY),
            pl.BlockSpec(memory_space=pltpu.VMEM),
        ],
        out_specs=[pl.BlockSpec(memory_space=pltpu.VMEM)] * 3,
        scratch_shapes=[
            pltpu.VMEM((capacity, width, wide), BF),
            pltpu.VMEM((half, width, lanes), BF),
            pltpu.VMEM((half, width, lanes), BF),
            pltpu.VMEM((half, width, lanes), BF),
            pltpu.VMEM((capacity, width, lanes), BF),
            pltpu.VMEM((capacity, width, lanes), BF),
            pltpu.VMEM((capacity, width, lanes), BF),
            pltpu.VMEM((3, slots + 1, 2, 16, lanes), BF),
            pltpu.VMEM((capacity * width, tile), BF),
            pltpu.VMEM((capacity * width, tile), BF),
            pltpu.VMEM((tile, tile), F32),
            pltpu.VMEM((3, AGG_DEV, width, tile), BF),
            pltpu.VMEM((3, AGG_DEV, width, tile), BF),
            pltpu.SemaphoreType.DMA((pieces,)),
            pltpu.SemaphoreType.DMA((2,)),
            pltpu.SemaphoreType.DMA((2,)),
            pltpu.SemaphoreType.DMA((6,)),
            pltpu.SemaphoreType.DMA((6,)),
            pltpu.SemaphoreType.DMA((6, groups - 1)),
            pltpu.SemaphoreType.DMA((6, groups - 1)),
            pltpu.SemaphoreType.DMA((3,)),
        ],
        compiler_params=pltpu.CompilerParams(
            vmem_limit_bytes=48 * 2**20, collective_id=0, has_side_effects=True
        ),
    )(code, fine_matrix_blocks, prolongator)
    return jnp.concatenate([part.astype(F32) for part in result], axis=-1)


def solution(mesh):
    return jax.shard_map(
        local,
        mesh=mesh,
        in_specs=(
            P(("grp", "dom"), None, None),
            P(("grp", "dom"), None, None),
            P(("grp", "dom"), None),
            P(("grp", "dom"), None),
            P(("grp", "dom")),
        ),
        out_specs=P("dom", None, None),
        check_vma=False,
    )
```
